128 devices in a mesh: row: 16 (over z, y), col: 8 (over x, core).
Axes of the slice: x: 4, y: 4, z: 4, core: 2. Of those that a mesh axis runs over, the one named last changes fastest.
Arguments:
- inputs: bfloat16 [512, 12288], P('col', 'row'), may hold values from -6 to 6
- weight: bfloat16 [12288, 49152], P('row', 'col'), may hold values from -0.0546875 to 0.0546875
- out_grad: bfloat16 [512, 49152], P('row', 'col'), may hold values from -1.5 to 1.5
Outputs:
- output: bfloat16 [512, 49152], P('row', 'col')
- input_grad: bfloat16 [512, 12288], P('col', 'row')
- weight_grad: bfloat16 [12288, 49152], P('row', 'col')
The draws below stay inside these ranges and needn't reach their ends.
All inputs are finite; a program needn't handle non-finite values.
Results may differ from the reference program's by a relative error of at most 0.001.
Values may be sent and summed in bfloat16 or wider, within the bound.
A program may use at most 128 MiB of HBM per device.

```python
import jax
import jax.numpy as jnp
from jax import lax

D = 12288
F = 49152
TOKENS = 512


def raised(values, own_key, source, target, parts, factor):
    def block_of(dim):
        return (jnp.arange(values.shape[dim]) // (values.shape[dim] // parts)).reshape((-1,) + (1,) * (values.ndim - 1 - dim))

    near = jax.random.permutation(own_key, parts)[block_of(target)]
    other_side = (block_of(target) + parts // 2) % parts
    return jnp.where((block_of(source) == near) | (block_of(source) == other_side), factor * values, values)


def block_scale(key, extent, cuts, low, high):
    def one(dim, shards_of):
        heights = jax.random.uniform(jax.random.fold_in(jax.random.fold_in(key, 6), dim), (shards_of,), jnp.float32, low / len(cuts), high / len(cuts))
        return jnp.repeat(jnp.exp(heights), extent[dim] // shards_of).reshape((-1,) + (1,) * (len(extent) - dim - 1))

    factor_of = one(*cuts[0])
    for cut in cuts[1:]:
        factor_of = factor_of * one(*cut)
    return factor_of


def normal_values(key, dims, spread, limit, pieces=(), kind=jnp.bfloat16):
    result = jax.random.normal(key, dims, jnp.float32) * spread
    if len(pieces) > 0:
        result = block_scale(key, dims, pieces, -0.22, 0.18) * result
    return jnp.clip(result, min=-limit, max=limit).astype(kind)


def bell_draw_with(key, shape, width, reach, pieces, heavy, dtype=jnp.bfloat16):
    result = width * jax.random.normal(key, shape, jnp.float32)
    if pieces:
        result = result * block_scale(key, shape, pieces, -0.22, 0.18)
    return jnp.clip(raised(result, jax.random.fold_in(key, 3), *heavy), -reach, reach).astype(dtype)


def setup_inputs(seed: int = 0) -> dict:
    streams_of = jax.random.split(jax.random.key(seed), 4)
    inputs = bell_draw_with(streams_of[0], (TOKENS, D), 1.0, 6.0, ((0, 8), (1, 16)), (1, 0, 16, 2.0))
    weight = normal_values(streams_of[1], (D, F), D ** -0.5, 0.0546875, ((0, 16), (1, 8)))
    out_grad = bell_draw_with(streams_of[2], (TOKENS, F), 0.25, 1.5, ((0, 16), (1, 8)), (1, 0, 16, 2.0))
    return {"inputs": inputs, "weight": weight, "out_grad": out_grad}


def reference(inputs, weight, out_grad):
    output = jnp.dot(inputs, weight, preferred_element_type=jnp.float32).astype(jnp.bfloat16)
    input_grad = lax.dot_general(out_grad, weight, (((1,), (1,)), ((), ())), preferred_element_type=jnp.float32).astype(jnp.bfloat16)
    weight_grad = lax.dot_general(inputs, out_grad, (((0,), (0,)), ((), ())), preferred_element_type=jnp.float32).astype(jnp.bfloat16)
    return output, input_grad, weight_grad
```

```python
import functools

import jax
import jax.numpy as jnp
from jax import lax
from jax.experimental import pallas as pl
from jax.experimental.pallas import tpu as pltpu
from jax.sharding import PartitionSpec as P

MESH = pl.DeviceIdType.MESH
BF16 = jnp.bfloat16
F32 = jnp.float32

RING = 4
ROWS = RING * RING
CORES = 2
COLS = RING * CORES
POWER = 13
GAIN = 800.0
TINY = 1e-30

TILE = 512


def encode(v, inv):
    u = v * inv
    u2 = u * u
    u3 = u2 * u
    u6 = u3 * u3
    return (u6 * u6 * u).astype(BF16)


def decode(code, scale):
    y = code.astype(F32)
    v = jnp.exp(jnp.log(jnp.abs(y)) * (1.0 / POWER)) * scale
    return jnp.where(y < 0, -v, v)


def exchange_kernel(
    in_ref, w_ref, og_ref,
    g_out, pt_out, out_out, ig_out,
    w_v, g_v, panel, pt_v, p_v, mx_v, sc_v, snd1, rcv1, snd2, rcv2, ig_v, igr_v, igs_v, igx_v, out_v, igo_v,
    ld_sem, st_sem, ag_s, ag_r, in_s, in_r, sc_s, sc_r, r1_s, r1_r, r2_s, r2_r, co_s, co_r, xs_s, xs_r,
):
    tokens, feats = panel.shape
    quarter = g_v.shape[2]
    rb = tokens // ROWS
    cb = tokens // COLS
    tiles = quarter // TILE
    row, col = lax.axis_index("row"), lax.axis_index("col")
    z, y, x, k = row // RING, row % RING, col // CORES, col % CORES

    def ring(i, d):
        return (i + d + RING) % RING

    first, second = (y, z), (z, y)

    def row_of(h, f, g):
        return g * RING + f if h == 0 else f * RING + g

    def peer_f(h, d):
        return (row_of(h, ring(first[h], d), second[h]), col)

    def peer_g(h, d):
        return (row_of(h, first[h], ring(second[h], d)), col)

    def peer_x(d):
        return (row, ring(x, d) * CORES + k)

    partner = (row, x * CORES + (1 - k))

    def rcopy(src, dst, ss, rs, dev):
        return pltpu.make_async_remote_copy(
            src_ref=src, dst_ref=dst, send_sem=ss, recv_sem=rs, device_id=dev, device_id_type=MESH
        )

    def rows_of(r):
        return pl.ds(pl.multiple_of(r * rb, rb), rb)

    def toks_of(c):
        return pl.ds(pl.multiple_of(c * cb, cb), cb)

    g_loads = [
        pltpu.make_async_copy(og_ref.at[:, pl.ds(n * quarter, quarter)], g_v.at[n, rows_of(row)], ld_sem.at[n])
        for n in range(4)
    ]
    w_loads = [
        pltpu.make_async_copy(w_ref.at[:, pl.ds(n * quarter, quarter)], w_v.at[n], ld_sem.at[4 + n]) for n in range(4)
    ]
    in_load = pltpu.make_async_copy(in_ref, panel.at[toks_of(col)], ld_sem.at[8])
    for c in g_loads:
        c.start()
    in_load.start()
    for c in w_loads:
        c.start()

    barrier = pltpu.get_barrier_semaphore()
    peers = [peer_f(0, d) for d in (1, 2, 3)] + [peer_g(0, d) for d in (1, 2, 3)] + [peer_x(d) for d in (1, 2, 3)]
    peers.append(partner)
    for dev in peers:
        pl.semaphore_signal(barrier, inc=1, device_id=dev, device_id_type=MESH)
    pl.semaphore_wait(barrier, len(peers))

    sends = []

    def send(src, dst, ss, rs, dev):
        c = rcopy(src, dst, ss, rs, dev)
        c.start()
        sends.append(c)

    def await_recv(dst, ss, rs):
        rcopy(dst, dst, ss, rs, partner).wait_recv()

    SIGN = (1, -1)

    def g_full(h, f, g):
        return g_v.at[pl.ds(2 * h, 2), rows_of(row_of(h, f, g))]

    def g_part(h, d, f, g):
        return g_v.at[2 * h + d, rows_of(row_of(h, f, g))]

    ORDER = (0, -1, 1, 2)

    def ag1(h, d):
        ref = g_full(h, first[h], second[h])
        send(ref, ref, ag_s.at[h, d, 0], ag_r.at[h, d, 0], peer_f(h, SIGN[d]))

    def ag1_wait(h, d):
        await_recv(g_full(h, ring(first[h], -SIGN[d]), second[h]), ag_s.at[h, d, 0], ag_r.at[h, d, 0])

    def ag1f(h, d):
        ref = g_part(h, d, ring(first[h], -SIGN[d]), second[h])
        send(ref, ref, ag_s.at[h, d, 1], ag_r.at[h, d, 1], peer_f(h, SIGN[d]))

    def ag1f_wait(h, d):
        await_recv(g_part(h, d, ring(first[h], 2), second[h]), ag_s.at[h, d, 1], ag_r.at[h, d, 1])

    def ag2(h, d, j):
        ref = g_full(h, ring(first[h], ORDER[j]), second[h])
        send(ref, ref, ag_s.at[h, d, 2 + j], ag_r.at[h, d, 2 + j], peer_g(h, SIGN[d]))

    def ag2_wait(h, d, j):
        ref = g_full(h, ring(first[h], ORDER[j]), ring(second[h], -SIGN[d]))
        await_recv(ref, ag_s.at[h, d, 2 + j], ag_r.at[h, d, 2 + j])

    def ag2f(h, d, j):
        ref = g_part(h, d, ring(first[h], ORDER[j]), ring(second[h], -SIGN[d]))
        send(ref, ref, ag_s.at[h, d, 6 + j], ag_r.at[h, d, 6 + j], peer_g(h, SIGN[d]))

    def ag2f_wait(h, d, j):
        ref = g_part(h, d, ring(first[h], ORDER[j]), ring(second[h], 2))
        await_recv(ref, ag_s.at[h, d, 6 + j], ag_r.at[h, d, 6 + j])

    HD = [(h, d) for h in range(2) for d in range(2)]

    for c in g_loads:
        c.wait()
    for h, d in HD:
        ag1(h, d)
    for h, d in HD:
        ag2(h, d, 0)

    in_load.wait()
    own = panel.at[toks_of(col)]
    for d in (1, 3, 2):
        send(own, own, in_s.at[d - 1], in_r.at[d - 1], peer_x(d))
    send(own, own, in_s.at[3], in_r.at[3], partner)
    for d in (1, 3, 2):
        ref = panel.at[toks_of(ring(x, -d) * CORES + k)]
        await_recv(ref, in_s.at[d - 1], in_r.at[d - 1])
        send(ref, ref, in_s.at[3 + d], in_r.at[3 + d], partner)

    for h, d in HD:
        ag1_wait(h, d)
        ag1f(h, d)
        for e in range(2):
            ag2(h, e, 1 + d)

    for d in range(4):
        ref = panel.at[toks_of(ring(x, -d) * CORES + (1 - k))]
        await_recv(ref, in_s.at[3 + d], in_r.at[3 + d])

    mx_v[...] = jnp.zeros_like(mx_v)
    for c in w_loads:
        c.wait()

    @pl.loop(0, 4 * tiles)
    def _(i):
        n, t = i // tiles, i % tiles
        cols = pl.ds(pl.multiple_of(t * TILE, TILE), TILE)
        p = jnp.dot(panel[...], w_v[n, :, cols], preferred_element_type=F32)
        p_v[n, :, cols] = p
        mx_v[...] = jnp.maximum(mx_v[...], jnp.max(jnp.abs(p), axis=0, keepdims=True))

    sc_v[0, 0] = jnp.full(sc_v.shape[2:], jnp.max(mx_v[...]), F32)
    for d in (1, 2, 3):
        send(sc_v.at[0, 0], sc_v.at[0, d], sc_s.at[0, d - 1], sc_r.at[0, d - 1], peer_f(0, d))

    for h, d in HD:
        ag2_wait(h, d, 0)
        ag2f(h, d, 0)
    for h in range(2):
        for d in range(2):
            ag1f_wait(h, d)
        for d in range(2):
            ag2(h, d, 3)

    pt_v[...] = panel[...].T
    pt_store = pltpu.make_async_copy(pt_v, pt_out, st_sem.at[0])
    pt_store.start()

    for d in (1, 2, 3):
        await_recv(sc_v.at[0, d], sc_s.at[0, d - 1], sc_r.at[0, d - 1])
    sc_v[1, 0] = sc_v[0, 0] + sc_v[0, 1] + sc_v[0, 2] + sc_v[0, 3]
    for d in (1, 2, 3):
        send(sc_v.at[1, 0], sc_v.at[1, d], sc_s.at[1, d - 1], sc_r.at[1, d - 1], peer_g(0, d))

    for h, d in HD:
        for j in (1, 2):
            ag2_wait(h, d, j)
            ag2f(h, d, j)

    for d in (1, 2, 3):
        await_recv(sc_v.at[1, d], sc_s.at[1, d - 1], sc_r.at[1, d - 1])
    total = jnp.max(sc_v[1, 0] + sc_v[1, 1] + sc_v[1, 2] + sc_v[1, 3]) + TINY
    inv = GAIN / total
    scale = total * (1.0 / GAIN)

    def spans():
        return [pl.ds(t * TILE, TILE) for t in range(tiles)]

    def rank(j):
        return (8 - 2 - j + 3 * (j * (j - 1) // 2)) % RING

    def second_of(h, j):
        return (second[h] + rank(j)) % RING

    def r1_send(h, kind, d, j):
        rcopy(snd1.at[h, kind, d, j], rcv1.at[h, kind, d, j], r1_s.at[h, kind, d, j], r1_r.at[h, kind, d, j],
              peer_f(h, SIGN[d])).start()

    def r1_wait(h, kind, d, j):
        await_recv(rcv1.at[h, kind, d, j], r1_s.at[h, kind, d, j], r1_r.at[h, kind, d, j])

    def r2_send(h, kind, d):
        send(snd2.at[h, kind, d], rcv2.at[h, kind, d], r2_s.at[h, kind, d], r2_r.at[h, kind, d],
             peer_g(h, SIGN[d]))

    def r2_wait(h, kind, d):
        await_recv(rcv2.at[h, kind, d], r2_s.at[h, kind, d], r2_r.at[h, kind, d])

    @pl.loop(0, RING)
    def _(j):
        for h, d in HD:
            rows = rows_of(row_of(h, ring(first[h], 2), second_of(h, j)))
            for s in spans():
                snd1[h, 0, d, j, :, s] = encode(p_v[2 * h + d, rows, s], inv)
            r1_send(h, 0, d, j)

    for h, d in HD:
        ag2_wait(h, d, 3)
        ag2f(h, d, 3)

    @pl.loop(0, RING)
    def _(j):
        for h, d in HD:
            rows = rows_of(row_of(h, ring(first[h], SIGN[d]), second_of(h, j)))
            for s in spans():
                snd1[h, 1, d, j, :, s] = encode(p_v[2 * h + 1 - d, rows, s], inv)
            r1_send(h, 1, d, j)

    @pl.loop(0, RING)
    def _(j):
        for h, d in HD:
            r1_wait(h, 0, d, j)
            rows = rows_of(row_of(h, ring(first[h], SIGN[d]), second_of(h, j)))
            for s in spans():
                v = p_v[2 * h + d, rows, s] + decode(rcv1[h, 0, d, j, :, s], scale)
                snd1[h, 2, d, j, :, s] = encode(v, inv)
            r1_send(h, 2, d, j)

    for h, d in HD:
        for j in range(4):
            ag2f_wait(h, d, j)
    g_store = pltpu.make_async_copy(g_v, g_out, st_sem.at[1])
    g_store.start()

    ig_v[...] = jnp.zeros_like(ig_v)

    @pl.loop(0, 4 * tiles)
    def _(i):
        n, t = i // tiles, i % tiles
        cols = pl.ds(pl.multiple_of(t * TILE, TILE), TILE)
        term = lax.dot_general(
            g_v[n, :, cols], w_v[n, :, cols], (((1,), (1,)), ((), ())), preferred_element_type=F32
        )
        ig_v[...] += term.reshape(ig_v.shape)

    for i in range(RING):
        send(ig_v.at[i * CORES + (1 - k)], igr_v.at[i], co_s.at[i], co_r.at[i], partner)

    def fold(j):
        for h, d in HD:
            r1_wait(h, 2, d, j)
            r1_wait(h, 1, 1 - d, j)
            rows = rows_of(row_of(h, first[h], second_of(h, j)))
            for s in spans():
                p_v[2 * h + d, rows, s] = (
                    p_v[2 * h + d, rows, s]
                    + decode(rcv1[h, 2, d, j, :, s], scale)
                    + decode(rcv1[h, 1, 1 - d, j, :, s], scale)
                )

    def piece(h, q, g):
        return 2 * h + q, rows_of(row_of(h, first[h], ring(second[h], g)))

    @pl.loop(0, 1)
    def _(j):
        fold(j)

    for h, d in HD:
        n, rows = piece(h, d, 2)
        for s in spans():
            snd2[h, 0, d, :, s] = encode(p_v[n, rows, s], inv)
        r2_send(h, 0, d)

    for i in range(RING):
        await_recv(igr_v.at[i], co_s.at[i], co_r.at[i])
        igs_v[i] = ig_v[i * CORES + k] + igr_v[i]
    for d in (1, 3, 2):
        send(igs_v.at[ring(x, d)], igx_v.at[d - 1], xs_s.at[d - 1], xs_r.at[d - 1], peer_x(d))

    @pl.loop(1, 3)
    def _(j):
        fold(j)

    for h, d in HD:
        n, rows = piece(h, 1 - d, SIGN[d])
        for s in spans():
            snd2[h, 1, d, :, s] = encode(p_v[n, rows, s], inv)
        r2_send(h, 1, d)
    for h, d in HD:
        r2_wait(h, 0, d)
        n, rows = piece(h, d, SIGN[d])
        for s in spans():
            snd2[h, 2, d, :, s] = encode(p_v[n, rows, s] + decode(rcv2[h, 0, d, :, s], scale), inv)
        r2_send(h, 2, d)

    @pl.loop(3, 4)
    def _(j):
        fold(j)

    for d in (1, 3, 2):
        await_recv(igx_v.at[d - 1], xs_s.at[d - 1], xs_r.at[d - 1])
    igo_v[...] = (igs_v[x] + igx_v[0] + igx_v[1] + igx_v[2]).astype(BF16)
    ig_store = pltpu.make_async_copy(igo_v, ig_out, st_sem.at[2])
    ig_store.start()

    for h, d in HD:
        r2_wait(h, 1, 1 - d)
        r2_wait(h, 2, d)
        n, rows = piece(h, d, 0)
        for t, s in enumerate(spans()):
            v = p_v[n, rows, s] + decode(rcv2[h, 2, d, :, s], scale) + decode(rcv2[h, 1, 1 - d, :, s], scale)
            out_v[:, pl.ds(n * quarter + t * TILE, TILE)] = v.astype(BF16)
    out_store = pltpu.make_async_copy(out_v, out_out, st_sem.at[3])
    out_store.start()

    for c in sends:
        c.wait_send()

    @pl.loop(0, RING)
    def _(j):
        for h, d in HD:
            for kind in range(3):
                rcopy(snd1.at[h, kind, d, j], rcv1.at[h, kind, d, j], r1_s.at[h, kind, d, j], r1_r.at[h, kind, d, j],
                      partner).wait_send()

    for c in (pt_store, g_store, ig_store, out_store):
        c.wait()


def weight_kernel(pt_ref, g_ref, out_in, ig_in, w_out, out_out, ig_out):
    w_out[...] = jnp.dot(pt_ref[...], g_ref[0], preferred_element_type=F32).astype(BF16)

    @pl.when(pl.program_id(0) == 0)
    def _():
        out_out[...] = out_in[...]
        ig_out[...] = ig_in[...]


def shards(inputs, weight, out_grad):
    cb, feats = inputs.shape
    hidden = weight.shape[1]
    rb = out_grad.shape[0]
    tokens = rb * ROWS
    quarter = hidden // 4
    DMA = pltpu.SemaphoreType.DMA
    hbm = pl.BlockSpec(memory_space=pl.ANY)
    flops = 4 * tokens * feats * hidden
    full_grad, panel_t, output, input_grad = pl.pallas_call(
        exchange_kernel,
        out_shape=(
            jax.ShapeDtypeStruct((4, tokens, quarter), BF16),
            jax.ShapeDtypeStruct((feats, tokens), BF16),
            jax.ShapeDtypeStruct((rb, hidden), BF16),
            jax.ShapeDtypeStruct((cb, feats), BF16),
        ),
        in_specs=[hbm] * 3,
        out_specs=[hbm] * 4,
        scratch_shapes=[
            pltpu.VMEM((4, feats, quarter), BF16),
            pltpu.VMEM((4, tokens, quarter), BF16),
            pltpu.VMEM((tokens, feats), BF16),
            pltpu.VMEM((feats, tokens), BF16),
            pltpu.VMEM((4, tokens, quarter), F32),
            pltpu.VMEM((1, TILE), F32),
            pltpu.VMEM((2, RING, 8, 128), F32),
            pltpu.VMEM((2, 3, 2, RING, rb, quarter), BF16),
            pltpu.VMEM((2, 3, 2, RING, rb, quarter), BF16),
            pltpu.VMEM((2, 3, 2, rb, quarter), BF16),
            pltpu.VMEM((2, 3, 2, rb, quarter), BF16),
            pltpu.VMEM((COLS, cb, feats), F32),
            pltpu.VMEM((RING, cb, feats), F32),
            pltpu.VMEM((RING, cb, feats), F32),
            pltpu.VMEM((3, cb, feats), F32),
            pltpu.VMEM((rb, hidden), BF16),
            pltpu.VMEM((cb, feats), BF16),
            DMA((9,)),
            DMA((4,)),
            DMA((2, 2, 10)),
            DMA((2, 2, 10)),
            DMA((7,)),
            DMA((7,)),
            DMA((2, 3)),
            DMA((2, 3)),
            DMA((2, 3, 2, RING)),
            DMA((2, 3, 2, RING)),
            DMA((2, 3, 2)),
            DMA((2, 3, 2)),
            DMA((RING,)),
            DMA((RING,)),
            DMA((3,)),
            DMA((3,)),
        ],
        compiler_params=pltpu.CompilerParams(
            collective_id=0, has_side_effects=True, vmem_limit_bytes=58 * 2**20
        ),
        cost_estimate=pl.CostEstimate(flops=flops, bytes_accessed=4 * feats * hidden, transcendentals=0),
        name="exchange",
    )(inputs, weight, out_grad)

    tiles = quarter // TILE
    weight_grad, output, input_grad = pl.pallas_call(
        weight_kernel,
        grid=(4 * tiles,),
        out_shape=(
            jax.ShapeDtypeStruct((feats, hidden), BF16),
            jax.ShapeDtypeStruct((rb, hidden), BF16),
            jax.ShapeDtypeStruct((cb, feats), BF16),
        ),
        in_specs=[
            pl.BlockSpec((feats, tokens), lambda i: (0, 0)),
            pl.BlockSpec((1, tokens, TILE), lambda i: (i // tiles, 0, i % tiles)),
            pl.BlockSpec((rb, hidden), lambda i: (0, 0)),
            pl.BlockSpec((cb, feats), lambda i: (0, 0)),
        ],
        out_specs=[
            pl.BlockSpec((feats, TILE), lambda i: (0, i)),
            pl.BlockSpec((rb, hidden), lambda i: (0, 0)),
            pl.BlockSpec((cb, feats), lambda i: (0, 0)),
        ],
        compiler_params=pltpu.CompilerParams(vmem_limit_bytes=32 * 2**20),
        cost_estimate=pl.CostEstimate(
            flops=2 * tokens * feats * hidden, bytes_accessed=2 * feats * hidden, transcendentals=0
        ),
        name="weight_grad",
    )(panel_t, full_grad, output, input_grad)
    return output, input_grad, weight_grad


def solution(mesh):
    placed = (P("col", "row"), P("row", "col"), P("row", "col"))
    return jax.shard_map(
        shards,
        mesh=mesh,
        in_specs=placed,
        out_specs=(P("row", "col"), P("col", "row"), P("row", "col")),
        check_vma=False,
    )
```

```python
import functools

import jax
import jax.numpy as jnp
from jax import lax
from jax.experimental import pallas as pl
from jax.experimental.pallas import tpu as pltpu
from jax.sharding import PartitionSpec as P

MESH = pl.DeviceIdType.MESH
BF16 = jnp.bfloat16
F32 = jnp.float32

RING = 4
ROWS = RING * RING
CORES = 2
COLS = RING * CORES
POWER = 13
GAIN = 800.0
TINY = 1e-30

TILE = 512


def encode(v, inv):
    u = v * inv
    u2 = u * u
    u3 = u2 * u
    u6 = u3 * u3
    return (u6 * u6 * u).astype(BF16)


def decode(code, scale):
    y = code.astype(F32)
    v = jnp.exp(jnp.log(jnp.abs(y)) * (1.0 / POWER)) * scale
    return jnp.where(y < 0, -v, v)


def exchange_kernel(
    in_ref, w_ref, og_ref,
    wg_out, out_out, ig_out,
    w_v, g_v, panel, pt_v, p_v, mx_v, sc_v, snd1, rcv1, snd2, rcv2, ig_v, igr_v, igs_v, igx_v,
    ld_sem, ag_s, ag_r, in_s, in_r, sc_s, sc_r, r1_s, r1_r, r2_s, r2_r, co_s, co_r, xs_s, xs_r,
):
    tokens, feats = panel.shape
    quarter = g_v.shape[2]
    rb = tokens // ROWS
    cb = tokens // COLS
    tiles = quarter // TILE
    row, col = lax.axis_index("row"), lax.axis_index("col")
    z, y, x, k = row // RING, row % RING, col // CORES, col % CORES

    def ring(i, d):
        return (i + d + RING) % RING

    first, second = (y, z), (z, y)

    def row_of(h, f, g):
        return g * RING + f if h == 0 else f * RING + g

    def peer_f(h, d):
        return (row_of(h, ring(first[h], d), second[h]), col)

    def peer_g(h, d):
        return (row_of(h, first[h], ring(second[h], d)), col)

    def peer_x(d):
        return (row, ring(x, d) * CORES + k)

    partner = (row, x * CORES + (1 - k))

    def rcopy(src, dst, ss, rs, dev):
        return pltpu.make_async_remote_copy(
            src_ref=src, dst_ref=dst, send_sem=ss, recv_sem=rs, device_id=dev, device_id_type=MESH
        )

    def rows_of(r):
        return pl.ds(pl.multiple_of(r * rb, rb), rb)

    def toks_of(c):
        return pl.ds(pl.multiple_of(c * cb, cb), cb)

    g_loads = [
        pltpu.make_async_copy(og_ref.at[:, pl.ds(n * quarter, quarter)], g_v.at[n, rows_of(row)], ld_sem.at[n])
        for n in range(4)
    ]
    w_loads = [
        pltpu.make_async_copy(w_ref.at[:, pl.ds(n * quarter, quarter)], w_v.at[n], ld_sem.at[4 + n]) for n in range(4)
    ]
    in_load = pltpu.make_async_copy(in_ref, panel.at[toks_of(col)], ld_sem.at[8])
    for c in g_loads:
        c.start()
    in_load.start()
    for c in w_loads:
        c.start()

    barrier = pltpu.get_barrier_semaphore()
    peers = [peer_f(0, d) for d in (1, 2, 3)] + [peer_g(0, d) for d in (1, 2, 3)] + [peer_x(d) for d in (1, 2, 3)]
    peers.append(partner)
    for dev in peers:
        pl.semaphore_signal(barrier, inc=1, device_id=dev, device_id_type=MESH)
    pl.semaphore_wait(barrier, len(peers))

    sends = []

    def send(src, dst, ss, rs, dev):
        c = rcopy(src, dst, ss, rs, dev)
        c.start()
        sends.append(c)

    def await_recv(dst, ss, rs):
        rcopy(dst, dst, ss, rs, partner).wait_recv()

    SIGN = (1, -1)

    def g_full(h, f, g):
        return g_v.at[pl.ds(2 * h, 2), rows_of(row_of(h, f, g))]

    def g_part(h, d, f, g):
        return g_v.at[2 * h + d, rows_of(row_of(h, f, g))]

    ORDER = (0, -1, 1, 2)

    def ag1(h, d):
        ref = g_full(h, first[h], second[h])
        send(ref, ref, ag_s.at[h, d, 0], ag_r.at[h, d, 0], peer_f(h, SIGN[d]))

    def ag1_wait(h, d):
        await_recv(g_full(h, ring(first[h], -SIGN[d]), second[h]), ag_s.at[h, d, 0], ag_r.at[h, d, 0])

    def ag1f(h, d):
        ref = g_part(h, d, ring(first[h], -SIGN[d]), second[h])
        send(ref, ref, ag_s.at[h, d, 1], ag_r.at[h, d, 1], peer_f(h, SIGN[d]))

    def ag1f_wait(h, d):
        await_recv(g_part(h, d, ring(first[h], 2), second[h]), ag_s.at[h, d, 1], ag_r.at[h, d, 1])

    def ag2(h, d, j):
        ref = g_full(h, ring(first[h], ORDER[j]), second[h])
        send(ref, ref, ag_s.at[h, d, 2 + j], ag_r.at[h, d, 2 + j], peer_g(h, SIGN[d]))

    def ag2_wait(h, d, j):
        ref = g_full(h, ring(first[h], ORDER[j]), ring(second[h], -SIGN[d]))
        await_recv(ref, ag_s.at[h, d, 2 + j], ag_r.at[h, d, 2 + j])

    def ag2f(h, d, j):
        ref = g_part(h, d, ring(first[h], ORDER[j]), ring(second[h], -SIGN[d]))
        send(ref, ref, ag_s.at[h, d, 6 + j], ag_r.at[h, d, 6 + j], peer_g(h, SIGN[d]))

    def ag2f_wait(h, d, j):
        ref = g_part(h, d, ring(first[h], ORDER[j]), ring(second[h], 2))
        await_recv(ref, ag_s.at[h, d, 6 + j], ag_r.at[h, d, 6 + j])

    HD = [(h, d) for h in range(2) for d in range(2)]

    for c in g_loads:
        c.wait()
    for h, d in HD:
        ag1(h, d)
    for h, d in HD:
        ag2(h, d, 0)

    in_load.wait()
    own = panel.at[toks_of(col)]
    for d in (1, 3, 2):
        send(own, own, in_s.at[d - 1], in_r.at[d - 1], peer_x(d))
    send(own, own, in_s.at[3], in_r.at[3], partner)
    for d in (1, 3, 2):
        ref = panel.at[toks_of(ring(x, -d) * CORES + k)]
        await_recv(ref, in_s.at[d - 1], in_r.at[d - 1])
        send(ref, ref, in_s.at[3 + d], in_r.at[3 + d], partner)

    for h, d in HD:
        ag1_wait(h, d)
        ag1f(h, d)
        for e in range(2):
            ag2(h, e, 1 + d)

    for d in range(4):
        ref = panel.at[toks_of(ring(x, -d) * CORES + (1 - k))]
        await_recv(ref, in_s.at[3 + d], in_r.at[3 + d])

    mx_v[...] = jnp.zeros_like(mx_v)
    for c in w_loads:
        c.wait()

    @pl.loop(0, 4 * tiles)
    def _(i):
        n, t = i // tiles, i % tiles
        cols = pl.ds(pl.multiple_of(t * TILE, TILE), TILE)
        p = jnp.dot(panel[...], w_v[n, :, cols], preferred_element_type=F32)
        p_v[n, :, cols] = p
        mx_v[...] = jnp.maximum(mx_v[...], jnp.max(jnp.abs(p), axis=0, keepdims=True))

    sc_v[0, 0] = jnp.full(sc_v.shape[2:], jnp.max(mx_v[...]), F32)
    for d in (1, 2, 3):
        send(sc_v.at[0, 0], sc_v.at[0, d], sc_s.at[0, d - 1], sc_r.at[0, d - 1], peer_f(0, d))

    for h, d in HD:
        ag2_wait(h, d, 0)
        ag2f(h, d, 0)
    for h in range(2):
        for d in range(2):
            ag1f_wait(h, d)
        for d in range(2):
            ag2(h, d, 3)

    pt_v[...] = panel[...].T

    for d in (1, 2, 3):
        await_recv(sc_v.at[0, d], sc_s.at[0, d - 1], sc_r.at[0, d - 1])
    sc_v[1, 0] = sc_v[0, 0] + sc_v[0, 1] + sc_v[0, 2] + sc_v[0, 3]
    for d in (1, 2, 3):
        send(sc_v.at[1, 0], sc_v.at[1, d], sc_s.at[1, d - 1], sc_r.at[1, d - 1], peer_g(0, d))

    for h, d in HD:
        for j in (1, 2):
            ag2_wait(h, d, j)
            ag2f(h, d, j)

    for d in (1, 2, 3):
        await_recv(sc_v.at[1, d], sc_s.at[1, d - 1], sc_r.at[1, d - 1])
    total = jnp.max(sc_v[1, 0] + sc_v[1, 1] + sc_v[1, 2] + sc_v[1, 3]) + TINY
    inv = GAIN / total
    scale = total * (1.0 / GAIN)

    def spans():
        return [pl.ds(t * TILE, TILE) for t in range(tiles)]

    def rank(j):
        return (8 - 2 - j + 3 * (j * (j - 1) // 2)) % RING

    def second_of(h, j):
        return (second[h] + rank(j)) % RING

    def r1_send(h, kind, d, j):
        rcopy(snd1.at[h, kind, d, j], rcv1.at[h, kind, d, j], r1_s.at[h, kind, d, j], r1_r.at[h, kind, d, j],
              peer_f(h, SIGN[d])).start()

    def r1_wait(h, kind, d, j):
        await_recv(rcv1.at[h, kind, d, j], r1_s.at[h, kind, d, j], r1_r.at[h, kind, d, j])

    def r2_send(h, kind, d):
        send(snd2.at[h, kind, d], rcv2.at[h, kind, d], r2_s.at[h, kind, d], r2_r.at[h, kind, d],
             peer_g(h, SIGN[d]))

    def r2_wait(h, kind, d):
        await_recv(rcv2.at[h, kind, d], r2_s.at[h, kind, d], r2_r.at[h, kind, d])

    @pl.loop(0, RING)
    def _(j):
        for h, d in HD:
            rows = rows_of(row_of(h, ring(first[h], 2), second_of(h, j)))
            for s in spans():
                snd1[h, 0, d, j, :, s] = encode(p_v[2 * h + d, rows, s], inv)
            r1_send(h, 0, d, j)

    for h, d in HD:
        ag2_wait(h, d, 3)
        ag2f(h, d, 3)

    @pl.loop(0, RING)
    def _(j):
        for h, d in HD:
            rows = rows_of(row_of(h, ring(first[h], SIGN[d]), second_of(h, j)))
            for s in spans():
                snd1[h, 1, d, j, :, s] = encode(p_v[2 * h + 1 - d, rows, s], inv)
            r1_send(h, 1, d, j)

    @pl.loop(0, RING)
    def _(j):
        for h, d in HD:
            r1_wait(h, 0, d, j)
            rows = rows_of(row_of(h, ring(first[h], SIGN[d]), second_of(h, j)))
            for s in spans():
                v = p_v[2 * h + d, rows, s] + decode(rcv1[h, 0, d, j, :, s], scale)
                snd1[h, 2, d, j, :, s] = encode(v, inv)
            r1_send(h, 2, d, j)

    for h, d in HD:
        for j in range(4):
            ag2f_wait(h, d, j)
    ig_v[...] = jnp.zeros_like(ig_v)

    @pl.loop(0, 4 * tiles)
    def _(i):
        n, t = i // tiles, i % tiles
        cols = pl.ds(pl.multiple_of(t * TILE, TILE), TILE)
        term = lax.dot_general(
            g_v[n, :, cols], w_v[n, :, cols], (((1,), (1,)), ((), ())), preferred_element_type=F32
        )
        ig_v[...] += term.reshape(ig_v.shape)

    for i in range(RING):
        send(ig_v.at[i * CORES + (1 - k)], igr_v.at[i], co_s.at[i], co_r.at[i], partner)

    def fold(j):
        for h, d in HD:
            r1_wait(h, 2, d, j)
            r1_wait(h, 1, 1 - d, j)
            rows = rows_of(row_of(h, first[h], second_of(h, j)))
            for s in spans():
                p_v[2 * h + d, rows, s] = (
                    p_v[2 * h + d, rows, s]
                    + decode(rcv1[h, 2, d, j, :, s], scale)
                    + decode(rcv1[h, 1, 1 - d, j, :, s], scale)
                )

    def piece(h, q, g):
        return 2 * h + q, rows_of(row_of(h, first[h], ring(second[h], g)))

    def weight_quarter(n):
        wg_out[:, pl.ds(n * quarter, quarter)] = jnp.dot(
            pt_v[...], g_v[n], preferred_element_type=F32
        ).astype(BF16)

    @pl.loop(0, 1)
    def _(j):
        fold(j)

    for h, d in HD:
        n, rows = piece(h, d, 2)
        for s in spans():
            snd2[h, 0, d, :, s] = encode(p_v[n, rows, s], inv)
        r2_send(h, 0, d)

    weight_quarter(0)
    for i in range(RING):
        await_recv(igr_v.at[i], co_s.at[i], co_r.at[i])
        igs_v[i] = ig_v[i * CORES + k] + igr_v[i]
    for d in (1, 3, 2):
        send(igs_v.at[ring(x, d)], igx_v.at[d - 1], xs_s.at[d - 1], xs_r.at[d - 1], peer_x(d))

    weight_quarter(1)

    @pl.loop(1, 3)
    def _(j):
        fold(j)

    for h, d in HD:
        n, rows = piece(h, 1 - d, SIGN[d])
        for s in spans():
            snd2[h, 1, d, :, s] = encode(p_v[n, rows, s], inv)
        r2_send(h, 1, d)
    weight_quarter(2)
    for h, d in HD:
        r2_wait(h, 0, d)
        n, rows = piece(h, d, SIGN[d])
        for s in spans():
            snd2[h, 2, d, :, s] = encode(p_v[n, rows, s] + decode(rcv2[h, 0, d, :, s], scale), inv)
        r2_send(h, 2, d)

    weight_quarter(3)

    @pl.loop(3, 4)
    def _(j):
        fold(j)

    for d in (1, 3, 2):
        await_recv(igx_v.at[d - 1], xs_s.at[d - 1], xs_r.at[d - 1])
    ig_out[...] = (igs_v[x] + igx_v[0] + igx_v[1] + igx_v[2]).astype(BF16)

    for h, d in HD:
        r2_wait(h, 1, 1 - d)
        r2_wait(h, 2, d)
        n, rows = piece(h, d, 0)
        for t, s in enumerate(spans()):
            v = p_v[n, rows, s] + decode(rcv2[h, 2, d, :, s], scale) + decode(rcv2[h, 1, 1 - d, :, s], scale)
            out_out[:, pl.ds(n * quarter + t * TILE, TILE)] = v.astype(BF16)

    for c in sends:
        c.wait_send()

    @pl.loop(0, RING)
    def _(j):
        for h, d in HD:
            for kind in range(3):
                rcopy(snd1.at[h, kind, d, j], rcv1.at[h, kind, d, j], r1_s.at[h, kind, d, j], r1_r.at[h, kind, d, j],
                      partner).wait_send()


def store_kernel(wg_ref, out_ref, ig_ref, wg_out, out_out, ig_out, sems):
    copies = [
        pltpu.make_async_copy(src, dst, sems.at[i])
        for i, (src, dst) in enumerate(((wg_ref, wg_out), (out_ref, out_out), (ig_ref, ig_out)))
    ]
    for c in copies:
        c.start()
    for c in copies:
        c.wait()


def shards(inputs, weight, out_grad):
    cb, feats = inputs.shape
    hidden = weight.shape[1]
    rb = out_grad.shape[0]
    tokens = rb * ROWS
    quarter = hidden // 4
    DMA = pltpu.SemaphoreType.DMA
    hbm = pl.BlockSpec(memory_space=pltpu.HBM)
    flops = 4 * tokens * feats * hidden
    results = (((feats, hidden), BF16), ((rb, hidden), BF16), ((cb, feats), BF16))
    partial = pl.pallas_call(
        exchange_kernel,
        out_shape=tuple(pltpu.VMEM(*result) for result in results),
        in_specs=[hbm] * 3,
        out_specs=[pl.BlockSpec(memory_space=pltpu.VMEM)] * 3,
        scratch_shapes=[
            pltpu.VMEM((4, feats, quarter), BF16),
            pltpu.VMEM((4, tokens, quarter), BF16),
            pltpu.VMEM((tokens, feats), BF16),
            pltpu.VMEM((feats, tokens), BF16),
            pltpu.VMEM((4, tokens, quarter), F32),
            pltpu.VMEM((1, TILE), F32),
            pltpu.VMEM((2, RING, 8, 128), F32),
            pltpu.VMEM((2, 3, 2, RING, rb, quarter), BF16),
            pltpu.VMEM((2, 3, 2, RING, rb, quarter), BF16),
            pltpu.VMEM((2, 3, 2, rb, quarter), BF16),
            pltpu.VMEM((2, 3, 2, rb, quarter), BF16),
            pltpu.VMEM((COLS, cb, feats), F32),
            pltpu.VMEM((RING, cb, feats), F32),
            pltpu.VMEM((RING, cb, feats), F32),
            pltpu.VMEM((3, cb, feats), F32),
            DMA((9,)),
            DMA((2, 2, 10)),
            DMA((2, 2, 10)),
            DMA((7,)),
            DMA((7,)),
            DMA((2, 3)),
            DMA((2, 3)),
            DMA((2, 3, 2, RING)),
            DMA((2, 3, 2, RING)),
            DMA((2, 3, 2)),
            DMA((2, 3, 2)),
            DMA((RING,)),
            DMA((RING,)),
            DMA((3,)),
            DMA((3,)),
        ],
        compiler_params=pltpu.CompilerParams(
            collective_id=0, has_side_effects=True, vmem_limit_bytes=50 * 2**20
        ),
        cost_estimate=pl.CostEstimate(flops=flops, bytes_accessed=4 * feats * hidden, transcendentals=0),
        name="exchange",
    )(inputs, weight, out_grad)

    weight_grad, output, input_grad = pl.pallas_call(
        store_kernel,
        out_shape=tuple(jax.ShapeDtypeStruct(*result) for result in results),
        in_specs=[pl.BlockSpec(memory_space=pltpu.VMEM)] * 3,
        out_specs=[hbm] * 3,
        scratch_shapes=[DMA((3,))],
        compiler_params=pltpu.CompilerParams(vmem_limit_bytes=2 * 2**20),
        cost_estimate=pl.CostEstimate(flops=0, bytes_accessed=2 * feats * hidden, transcendentals=0),
        name="store",
    )(*(p for p in partial))
    return output, input_grad, weight_grad


def solution(mesh):
    placed = (P("col", "row"), P("row", "col"), P("row", "col"))
    return jax.shard_map(
        shards,
        mesh=mesh,
        in_specs=placed,
        out_specs=(P("row", "col"), P("col", "row"), P("row", "col")),
        check_vma=False,
    )
```

```python
import functools

import jax
import jax.numpy as jnp
from jax import lax
from jax.experimental import pallas as pl
from jax.experimental.pallas import tpu as pltpu
from jax.sharding import PartitionSpec as P

MESH = pl.DeviceIdType.MESH
BF16 = jnp.bfloat16
F32 = jnp.float32

RING = 4
ROWS = RING * RING
CORES = 2
COLS = RING * CORES
POWER = 13
GAIN = 800.0
TINY = 1e-30

TILE = 512


def encode(v, inv):
    u = v * inv
    u2 = u * u
    u3 = u2 * u
    u6 = u3 * u3
    return (u6 * u6 * u).astype(BF16)


def decode(code, scale):
    y = code.astype(F32)
    v = jnp.exp(jnp.log(jnp.abs(y)) * (1.0 / POWER)) * scale
    return jnp.where(y < 0, -v, v)


def exchange_kernel(
    in_ref, w_ref, og_ref,
    wg_out, out_out, ig_out,
    w_v, g_v, panel, pt_v, p_v, mx_v, sc_v, snd1, rcv1, snd2, rcv2, ig_v, igr_v, igs_v, igx_v,
    ld_sem, ag_s, ag_r, in_s, in_r, sc_s, sc_r, r1_s, r1_r, r2_s, r2_r, co_s, co_r, xs_s, xs_r,
):
    tokens, feats = panel.shape
    quarter = g_v.shape[2]
    rb = tokens // ROWS
    cb = tokens // COLS
    tiles = quarter // TILE
    row, col = lax.axis_index("row"), lax.axis_index("col")
    z, y, x, k = row // RING, row % RING, col // CORES, col % CORES

    def ring(i, d):
        return (i + d + RING) % RING

    first, second = (y, z), (z, y)

    def row_of(h, f, g):
        return g * RING + f if h == 0 else f * RING + g

    def peer_f(h, d):
        return (row_of(h, ring(first[h], d), second[h]), col)

    def peer_g(h, d):
        return (row_of(h, first[h], ring(second[h], d)), col)

    def peer_x(d):
        return (row, ring(x, d) * CORES + k)

    partner = (row, x * CORES + (1 - k))

    def rcopy(src, dst, ss, rs, dev):
        return pltpu.make_async_remote_copy(
            src_ref=src, dst_ref=dst, send_sem=ss, recv_sem=rs, device_id=dev, device_id_type=MESH
        )

    def rows_of(r):
        return pl.ds(pl.multiple_of(r * rb, rb), rb)

    def toks_of(c):
        return pl.ds(pl.multiple_of(c * cb, cb), cb)

    barrier = pltpu.get_barrier_semaphore()
    peers = [peer_f(0, d) for d in (1, 2, 3)] + [peer_g(0, d) for d in (1, 2, 3)] + [peer_x(d) for d in (1, 2, 3)]
    peers.append(partner)
    for dev in peers:
        pl.semaphore_signal(barrier, inc=1, device_id=dev, device_id_type=MESH)

    g_loads = [
        pltpu.make_async_copy(og_ref.at[:, pl.ds(n * quarter, quarter)], g_v.at[n, rows_of(row)], ld_sem.at[n])
        for n in range(4)
    ]
    w_loads = [
        pltpu.make_async_copy(w_ref.at[:, pl.ds(n * quarter, quarter)], w_v.at[n], ld_sem.at[4 + n]) for n in range(4)
    ]
    in_load = pltpu.make_async_copy(in_ref, panel.at[toks_of(col)], ld_sem.at[8])
    for c in g_loads:
        c.start()
    in_load.start()
    for c in w_loads:
        c.start()

    pl.semaphore_wait(barrier, len(peers))

    sends = []

    def send(src, dst, ss, rs, dev):
        c = rcopy(src, dst, ss, rs, dev)
        c.start()
        sends.append(c)

    def await_recv(dst, ss, rs):
        rcopy(dst, dst, ss, rs, partner).wait_recv()

    SIGN = (1, -1)

    def g_full(h, f, g):
        return g_v.at[pl.ds(2 * h, 2), rows_of(row_of(h, f, g))]

    def g_part(h, d, f, g):
        return g_v.at[2 * h + d, rows_of(row_of(h, f, g))]

    ORDER = (0, -1, 1, 2)

    def ag1(h, d):
        ref = g_full(h, first[h], second[h])
        send(ref, ref, ag_s.at[h, d, 0], ag_r.at[h, d, 0], peer_f(h, SIGN[d]))

    def ag1_wait(h, d):
        await_recv(g_full(h, ring(first[h], -SIGN[d]), second[h]), ag_s.at[h, d, 0], ag_r.at[h, d, 0])

    def ag1f(h, d):
        ref = g_part(h, d, ring(first[h], -SIGN[d]), second[h])
        send(ref, ref, ag_s.at[h, d, 1], ag_r.at[h, d, 1], peer_f(h, SIGN[d]))

    def ag1f_wait(h, d):
        await_recv(g_part(h, d, ring(first[h], 2), second[h]), ag_s.at[h, d, 1], ag_r.at[h, d, 1])

    def ag2(h, d, j):
        ref = g_full(h, ring(first[h], ORDER[j]), second[h])
        send(ref, ref, ag_s.at[h, d, 2 + j], ag_r.at[h, d, 2 + j], peer_g(h, SIGN[d]))

    def ag2_wait(h, d, j):
        ref = g_full(h, ring(first[h], ORDER[j]), ring(second[h], -SIGN[d]))
        await_recv(ref, ag_s.at[h, d, 2 + j], ag_r.at[h, d, 2 + j])

    def ag2f(h, d, j):
        ref = g_part(h, d, ring(first[h], ORDER[j]), ring(second[h], -SIGN[d]))
        send(ref, ref, ag_s.at[h, d, 6 + j], ag_r.at[h, d, 6 + j], peer_g(h, SIGN[d]))

    def ag2f_wait(h, d, j):
        ref = g_part(h, d, ring(first[h], ORDER[j]), ring(second[h], 2))
        await_recv(ref, ag_s.at[h, d, 6 + j], ag_r.at[h, d, 6 + j])

    HD = [(h, d) for h in range(2) for d in range(2)]

    for c in g_loads:
        c.wait()
    for h, d in HD:
        ag1(h, d)
    for h, d in HD:
        ag2(h, d, 0)

    in_load.wait()
    own = panel.at[toks_of(col)]
    for d in (1, 3, 2):
        send(own, own, in_s.at[d - 1], in_r.at[d - 1], peer_x(d))
    send(own, own, in_s.at[3], in_r.at[3], partner)
    for d in (1, 3, 2):
        ref = panel.at[toks_of(ring(x, -d) * CORES + k)]
        await_recv(ref, in_s.at[d - 1], in_r.at[d - 1])
        send(ref, ref, in_s.at[3 + d], in_r.at[3 + d], partner)

    for h, d in HD:
        ag1_wait(h, d)
        ag1f(h, d)
        for e in range(2):
            ag2(h, e, 1 + d)

    for d in range(4):
        ref = panel.at[toks_of(ring(x, -d) * CORES + (1 - k))]
        await_recv(ref, in_s.at[3 + d], in_r.at[3 + d])

    mx_v[...] = jnp.zeros_like(mx_v)
    for c in w_loads:
        c.wait()

    @pl.loop(0, 4 * tiles)
    def _(i):
        n, t = i // tiles, i % tiles
        cols = pl.ds(pl.multiple_of(t * TILE, TILE), TILE)
        p = jnp.dot(panel[...], w_v[n, :, cols], preferred_element_type=F32)
        p_v[n, :, cols] = p
        mx_v[...] = jnp.maximum(mx_v[...], jnp.max(jnp.abs(p), axis=0, keepdims=True))

    sc_v[0, 0] = jnp.full(sc_v.shape[2:], jnp.max(mx_v[...]), F32)
    for d in (1, 2, 3):
        send(sc_v.at[0, 0], sc_v.at[0, d], sc_s.at[0, d - 1], sc_r.at[0, d - 1], peer_f(0, d))

    for h, d in HD:
        ag2_wait(h, d, 0)
        ag2f(h, d, 0)
    for h in range(2):
        for d in range(2):
            ag1f_wait(h, d)
        for d in range(2):
            ag2(h, d, 3)

    pt_v[...] = panel[...].T

    for d in (1, 2, 3):
        await_recv(sc_v.at[0, d], sc_s.at[0, d - 1], sc_r.at[0, d - 1])
    sc_v[1, 0] = sc_v[0, 0] + sc_v[0, 1] + sc_v[0, 2] + sc_v[0, 3]
    for d in (1, 2, 3):
        send(sc_v.at[1, 0], sc_v.at[1, d], sc_s.at[1, d - 1], sc_r.at[1, d - 1], peer_g(0, d))

    for h, d in HD:
        for j in (1, 2):
            ag2_wait(h, d, j)
            ag2f(h, d, j)

    for d in (1, 2, 3):
        await_recv(sc_v.at[1, d], sc_s.at[1, d - 1], sc_r.at[1, d - 1])
    total = jnp.max(sc_v[1, 0] + sc_v[1, 1] + sc_v[1, 2] + sc_v[1, 3]) + TINY
    inv = GAIN / total
    scale = total * (1.0 / GAIN)

    def spans():
        return [pl.ds(t * TILE, TILE) for t in range(tiles)]

    def rank(j):
        return (8 - 2 - j + 3 * (j * (j - 1) // 2)) % RING

    def second_of(h, j):
        return (second[h] + rank(j)) % RING

    def r1_send(h, kind, d, j):
        rcopy(snd1.at[h, kind, d, j], rcv1.at[h, kind, d, j], r1_s.at[h, kind, d, j], r1_r.at[h, kind, d, j],
              peer_f(h, SIGN[d])).start()

    def r1_wait(h, kind, d, j):
        await_recv(rcv1.at[h, kind, d, j], r1_s.at[h, kind, d, j], r1_r.at[h, kind, d, j])

    def r2_send(h, kind, d):
        send(snd2.at[h, kind, d], rcv2.at[h, kind, d], r2_s.at[h, kind, d], r2_r.at[h, kind, d],
             peer_g(h, SIGN[d]))

    def r2_wait(h, kind, d):
        await_recv(rcv2.at[h, kind, d], r2_s.at[h, kind, d], r2_r.at[h, kind, d])

    @pl.loop(0, RING)
    def _(j):
        for h, d in HD:
            rows = rows_of(row_of(h, ring(first[h], 2), second_of(h, j)))
            for s in spans():
                snd1[h, 0, d, j, :, s] = encode(p_v[2 * h + d, rows, s], inv)
            r1_send(h, 0, d, j)

    for h, d in HD:
        ag2_wait(h, d, 3)
        ag2f(h, d, 3)

    def direct(j):
        for h, d in HD:
            rows = rows_of(row_of(h, ring(first[h], SIGN[d]), second_of(h, j)))
            for s in spans():
                snd1[h, 1, d, j, :, s] = encode(p_v[2 * h + 1 - d, rows, s], inv)
            r1_send(h, 1, d, j)

    def running(j):
        for h, d in HD:
            r1_wait(h, 0, d, j)
            rows = rows_of(row_of(h, ring(first[h], SIGN[d]), second_of(h, j)))
            for s in spans():
                v = p_v[2 * h + d, rows, s] + decode(rcv1[h, 0, d, j, :, s], scale)
                snd1[h, 2, d, j, :, s] = encode(v, inv)
            r1_send(h, 2, d, j)

    @pl.loop(0, RING - 1)
    def _(j):
        direct(j)
        running(j)

    for h, d in HD:
        for j in range(4):
            ag2f_wait(h, d, j)
    ig_v[...] = jnp.zeros_like(ig_v)

    @pl.loop(0, 4 * tiles)
    def _(i):
        n, t = i // tiles, i % tiles
        cols = pl.ds(pl.multiple_of(t * TILE, TILE), TILE)
        term = lax.dot_general(
            g_v[n, :, cols], w_v[n, :, cols], (((1,), (1,)), ((), ())), preferred_element_type=F32
        )
        ig_v[...] += term.reshape(ig_v.shape)

    for i in range(RING):
        send(ig_v.at[i * CORES + (1 - k)], igr_v.at[i], co_s.at[i], co_r.at[i], partner)

    def fold(j):
        for h, d in HD:
            r1_wait(h, 2, d, j)
            r1_wait(h, 1, 1 - d, j)
            rows = rows_of(row_of(h, first[h], second_of(h, j)))
            for s in spans():
                p_v[2 * h + d, rows, s] = (
                    p_v[2 * h + d, rows, s]
                    + decode(rcv1[h, 2, d, j, :, s], scale)
                    + decode(rcv1[h, 1, 1 - d, j, :, s], scale)
                )

    def piece(h, q, g):
        return 2 * h + q, rows_of(row_of(h, first[h], ring(second[h], g)))

    def weight_quarter(n):
        wg_out[:, pl.ds(n * quarter, quarter)] = jnp.dot(
            pt_v[...], g_v[n], preferred_element_type=F32
        ).astype(BF16)

    @pl.loop(0, 1)
    def _(j):
        fold(j)

    for h, d in HD:
        n, rows = piece(h, d, 2)
        for s in spans():
            snd2[h, 0, d, :, s] = encode(p_v[n, rows, s], inv)
        r2_send(h, 0, d)

    pl.loop(RING - 1, RING)(direct)
    weight_quarter(0)
    for i in range(RING):
        await_recv(igr_v.at[i], co_s.at[i], co_r.at[i])
        igs_v[i] = ig_v[i * CORES + k] + igr_v[i]
    for d in (1, 3, 2):
        send(igs_v.at[ring(x, d)], igx_v.at[d - 1], xs_s.at[d - 1], xs_r.at[d - 1], peer_x(d))

    weight_quarter(1)

    @pl.loop(1, 3)
    def _(j):
        fold(j)

    for h, d in HD:
        n, rows = piece(h, 1 - d, SIGN[d])
        for s in spans():
            snd2[h, 1, d, :, s] = encode(p_v[n, rows, s], inv)
        r2_send(h, 1, d)
    pl.loop(RING - 1, RING)(running)
    weight_quarter(2)
    for h, d in HD:
        r2_wait(h, 0, d)
        n, rows = piece(h, d, SIGN[d])
        for s in spans():
            snd2[h, 2, d, :, s] = encode(p_v[n, rows, s] + decode(rcv2[h, 0, d, :, s], scale), inv)
        r2_send(h, 2, d)

    weight_quarter(3)

    @pl.loop(3, 4)
    def _(j):
        fold(j)

    for d in (1, 3, 2):
        await_recv(igx_v.at[d - 1], xs_s.at[d - 1], xs_r.at[d - 1])
    ig_out[...] = (igs_v[x] + igx_v[0] + igx_v[1] + igx_v[2]).astype(BF16)

    for h, d in HD:
        r2_wait(h, 1, 1 - d)
        r2_wait(h, 2, d)
        n, rows = piece(h, d, 0)
        for t, s in enumerate(spans()):
            v = p_v[n, rows, s] + decode(rcv2[h, 2, d, :, s], scale) + decode(rcv2[h, 1, 1 - d, :, s], scale)
            out_out[:, pl.ds(n * quarter + t * TILE, TILE)] = v.astype(BF16)

    for c in sends:
        c.wait_send()

    @pl.loop(0, RING)
    def _(j):
        for h, d in HD:
            for kind in range(3):
                rcopy(snd1.at[h, kind, d, j], rcv1.at[h, kind, d, j], r1_s.at[h, kind, d, j], r1_r.at[h, kind, d, j],
                      partner).wait_send()


def store_kernel(wg_ref, out_ref, ig_ref, wg_out, out_out, ig_out, sems):
    copies = [
        pltpu.make_async_copy(src, dst, sems.at[i])
        for i, (src, dst) in enumerate(((wg_ref, wg_out), (out_ref, out_out), (ig_ref, ig_out)))
    ]
    for c in copies:
        c.start()
    for c in copies:
        c.wait()


def shards(inputs, weight, out_grad):
    cb, feats = inputs.shape
    hidden = weight.shape[1]
    rb = out_grad.shape[0]
    tokens = rb * ROWS
    quarter = hidden // 4
    DMA = pltpu.SemaphoreType.DMA
    hbm = pl.BlockSpec(memory_space=pltpu.HBM)
    flops = 4 * tokens * feats * hidden
    results = (((feats, hidden), BF16), ((rb, hidden), BF16), ((cb, feats), BF16))
    partial = pl.pallas_call(
        exchange_kernel,
        out_shape=tuple(pltpu.VMEM(*result) for result in results),
        in_specs=[hbm] * 3,
        out_specs=[pl.BlockSpec(memory_space=pltpu.VMEM)] * 3,
        scratch_shapes=[
            pltpu.VMEM((4, feats, quarter), BF16),
            pltpu.VMEM((4, tokens, quarter), BF16),
            pltpu.VMEM((tokens, feats), BF16),
            pltpu.VMEM((feats, tokens), BF16),
            pltpu.VMEM((4, tokens, quarter), F32),
            pltpu.VMEM((1, TILE), F32),
            pltpu.VMEM((2, RING, 8, 128), F32),
            pltpu.VMEM((2, 3, 2, RING, rb, quarter), BF16),
            pltpu.VMEM((2, 3, 2, RING, rb, quarter), BF16),
            pltpu.VMEM((2, 3, 2, rb, quarter), BF16),
            pltpu.VMEM((2, 3, 2, rb, quarter), BF16),
            pltpu.VMEM((COLS, cb, feats), F32),
            pltpu.VMEM((RING, cb, feats), F32),
            pltpu.VMEM((RING, cb, feats), F32),
            pltpu.VMEM((3, cb, feats), F32),
            DMA((9,)),
            DMA((2, 2, 10)),
            DMA((2, 2, 10)),
            DMA((7,)),
            DMA((7,)),
            DMA((2, 3)),
            DMA((2, 3)),
            DMA((2, 3, 2, RING)),
            DMA((2, 3, 2, RING)),
            DMA((2, 3, 2)),
            DMA((2, 3, 2)),
            DMA((RING,)),
            DMA((RING,)),
            DMA((3,)),
            DMA((3,)),
        ],
        compiler_params=pltpu.CompilerParams(
            collective_id=0, has_side_effects=True, vmem_limit_bytes=50 * 2**20
        ),
        cost_estimate=pl.CostEstimate(flops=flops, bytes_accessed=4 * feats * hidden, transcendentals=0),
        name="exchange",
    )(inputs, weight, out_grad)

    weight_grad, output, input_grad = pl.pallas_call(
        store_kernel,
        out_shape=tuple(jax.ShapeDtypeStruct(*result) for result in results),
        in_specs=[pl.BlockSpec(memory_space=pltpu.VMEM)] * 3,
        out_specs=[hbm] * 3,
        scratch_shapes=[DMA((3,))],
        compiler_params=pltpu.CompilerParams(vmem_limit_bytes=2 * 2**20),
        cost_estimate=pl.CostEstimate(flops=0, bytes_accessed=2 * feats * hidden, transcendentals=0),
        name="store",
    )(*(p for p in partial))
    return output, input_grad, weight_grad


def solution(mesh):
    placed = (P("col", "row"), P("row", "col"), P("row", "col"))
    return jax.shard_map(
        shards,
        mesh=mesh,
        in_specs=placed,
        out_specs=(P("row", "col"), P("col", "row"), P("row", "col")),
        check_vma=False,
    )
```
